256 devices in a mesh: space: 64 (over z, x, core), tm: 4 (over y).
Axes of the slice: x: 4, y: 4, z: 8, core: 2. Of those that a mesh axis runs over, the one named last changes fastest.
Arguments:
- archive: float32 [512, 524288], P('tm', 'space'), may hold values from -64 to 64
- leaf_sketch: float32 [128, 64], replicated, may hold values from -0.5 to 0.5
- merge_sketch: float32 [128, 64], replicated, may hold values from -0.5 to 0.5
Outputs:
- modes: float32 [64, 524288], P('tm', 'space')
The draws below stay inside these ranges and needn't reach their ends.
All inputs are finite; a program needn't handle non-finite values.
Results may differ from the reference program's by a relative error of at most 0.0003.
Values sent between devices are 32-bit elements; how exact they have to be, the bound alone decides.
No kernel may reach another device: no remote copies, remote signals or barrier semaphores. Data moves between devices by JAX's collectives and lax.ppermute only.
A program may use at most 192 MiB of HBM per device.

```python
import math
import jax
import jax.numpy as jnp
from jax import lax

SNAP_W = 128
R = 64
CELLS = 524288
SNAPS = 512
LEVELS = 2
N_TM = 4


def draw_archive(key, part):
    key = jax.random.fold_in(key, 7)
    subkeys = jax.random.split(key, 3)
    snap_scale = jnp.exp(jax.random.uniform(subkeys[0], (SNAPS, 1), jnp.float32, math.log(0.3), math.log(3.0)))
    cell_scale = jnp.exp(jax.random.uniform(subkeys[1], (1, CELLS), jnp.float32, math.log(0.3), math.log(3.0)))
    fluctuation = jax.random.truncated_normal(subkeys[2], -4.0, 4.0, (SNAPS, CELLS), jnp.float32)
    return fluctuation * snap_scale * cell_scale


def scatter_about(rng, shape, deviation, bound, kind=jnp.bfloat16):
    return jnp.clip(deviation * jax.random.normal(rng, shape, jnp.float32), -bound, bound).astype(kind)


def setup_inputs(seed: int = 0) -> dict:
    seeds = jax.random.split(jax.random.key(seed), 4)
    return {
        "archive": draw_archive(jax.random.fold_in(seeds[3], 71), 0),
        "leaf_sketch": scatter_about(seeds[1], (SNAP_W, R), SNAP_W ** -0.5, 0.5, jnp.float32),
        "merge_sketch": scatter_about(seeds[2], (2 * R, R), (2 * R) ** -0.5, 0.5, jnp.float32),
    }


def contract(former, latter):
    return lax.dot_general(former, latter, (((1,), (1,)), ((), ())), precision=lax.Precision.HIGHEST)

def merge_piece(stacked, sketch):
    highest = lax.Precision.HIGHEST
    gram_cells = contract(stacked, stacked)
    projected = jnp.dot(sketch.T, gram_cells, precision=highest)
    sketch_gram = jnp.dot(projected, sketch, precision=highest)
    lower_y = jnp.linalg.cholesky(sketch_gram)
    mixed_rows = jax.scipy.linalg.solve_triangular(lower_y, projected, lower=True)
    lower_k = jnp.linalg.cholesky(contract(mixed_rows, mixed_rows))
    weights = jax.scipy.linalg.solve_triangular(lower_y, sketch.T, lower=True)
    coeffs = jnp.dot(lower_k.T, weights, precision=highest)
    return jnp.dot(coeffs, stacked, precision=highest)

def reference(archive, leaf_sketch, merge_sketch):
    blocks = archive.reshape(N_TM, N_TM, SNAP_W // N_TM, CELLS)

    def leaf_piece(window_id):
        window = lax.dynamic_index_in_dim(blocks, window_id, 1, keepdims=False)
        window = jnp.transpose(window, (1, 0, 2)).reshape(SNAP_W, CELLS)
        return merge_piece(window, leaf_sketch)
    pieces = lax.map(leaf_piece, jnp.arange(N_TM, dtype=jnp.int32))

    def pair_piece(stacked):
        return merge_piece(stacked, merge_sketch)
    remain_count = N_TM
    for tier_index in range(LEVELS):
        paired = pieces.reshape(remain_count // 2, 2 * R, CELLS)
        pieces = lax.map(pair_piece, paired)
        remain_count = remain_count // 2
    return pieces[0]
```

```python
import functools

import jax
import jax.numpy as jnp
from jax import lax
from jax.experimental import pallas as pl
from jax.experimental.pallas import tpu as pltpu
from jax.sharding import Mesh, PartitionSpec as P

HI = lax.Precision.HIGHEST
SUB = 8
VMEM = pl.BlockSpec(memory_space=pltpu.VMEM)
SMEM = pl.BlockSpec(memory_space=pltpu.SMEM)
SPACE = ("z", "x", "core")
PARAMS = pltpu.CompilerParams(vmem_limit_bytes=40 * 2**20)


def mm(a, b):
    return jnp.dot(a, b, precision=HI, preferred_element_type=jnp.float32)


def mmt(a, b):
    return lax.dot_general(a, b, (((1,), (1,)), ((), ())), precision=HI, preferred_element_type=jnp.float32)


def mtm(a, b):
    return lax.dot_general(a, b, (((0,), (0,)), ((), ())), precision=HI, preferred_element_type=jnp.float32)


def eliminate(mats, width):
    n, lanes = mats[0].shape
    count = n // SUB
    rows = lax.broadcasted_iota(jnp.int32, (SUB, lanes), 0)
    work = [[m[b * SUB : (b + 1) * SUB, :] for b in range(count)] for m in mats]

    def row(v, c):
        return jnp.broadcast_to(v[c : c + 1, :], (SUB, lanes))

    for first in range(0, n, width):
        p, off = divmod(first, SUB)
        spread = [
            [
                {b: jnp.broadcast_to(w[b][:, first + c : first + c + 1], (SUB, lanes)) for b in range(p, count)}
                for c in range(width)
            ]
            for w in work
        ]
        for c in range(width):
            at = off + c
            for w, t in zip(work, spread):
                inverse = 1.0 / row(t[c][p], at)
                pivot_row = row(w[p], at) * inverse
                for later in range(c + 1, width):
                    scale = row(t[c][p], off + later) * inverse
                    for b in range(p, count):
                        t[later][b] = t[later][b] - t[c][b] * scale
                below = jnp.where(rows > at, t[c][p], 0.0)
                w[p] = w[p] - below * pivot_row
                for b in range(p + 1, count):
                    w[b] = w[b] - t[c][b] * pivot_row
                t[c]["d"] = row(t[c][p], at)
        for w, t in zip(work, spread):
            scale = None
            for c in range(width):
                d = t[c]["d"]
                scale = d if scale is None else jnp.where(rows >= off + c, d, scale)
            scaled = w[p] * lax.rsqrt(scale)
            w[p] = jnp.where((rows >= off) & (rows < off + width), scaled, w[p]) if width < SUB else scaled
    return [jnp.concatenate(w, 0) for w in work]


def upper(u):
    r = lax.broadcasted_iota(jnp.int32, u.shape, 0)
    c = lax.broadcasted_iota(jnp.int32, u.shape, 1)
    return jnp.where(c >= r, u, 0.0)


def level(bs, sketch, widths):
    rank = sketch.shape[1]
    eye = (
        lax.broadcasted_iota(jnp.int32, (rank, rank), 0) == lax.broadcasted_iota(jnp.int32, (rank, rank), 1)
    ).astype(jnp.float32)
    aug = [jnp.concatenate([mm(b, sketch), eye], 1) for b in bs]
    inv = [e[:, rank:] for e in eliminate(aug, widths[0])]
    mixed = [mm(i, b) for i, b in zip(inv, bs)]
    grams = [mmt(m, m) for m in mixed]
    fac = [upper(e) for e in eliminate(grams, widths[1])]
    return fac, [mm(f, i) for f, i in zip(fac, inv)]


def pair(fa, fb, cross):
    return jnp.concatenate(
        [jnp.concatenate([mmt(fa, fa), cross], 1), jnp.concatenate([cross.T, mmt(fb, fb)], 1)], 0
    )


def factor_kernel(widths, red_ref, leaf_ref, leaf_t_ref, merge_ref, merge_t_ref, out_ref):
    wl, wm, wmt = leaf_ref[...], merge_ref[...], merge_t_ref[...]
    r = wl.shape[1]
    leaves = [red_ref[w * r : (w + 1) * r, :] for w in range(4)]
    f, p = level(leaves, wl, widths[0])
    x01, x23 = red_ref[4 * r : 5 * r, :r], red_ref[4 * r : 5 * r, r:]
    cross = red_ref[5 * r : 7 * r, :]
    g = [
        pair(f[0], f[1], mmt(mm(p[0], x01), p[1])),
        pair(f[2], f[3], mmt(mm(p[2], x23), p[3])),
    ]
    f1, q1 = level([mm(wmt, x) for x in g], wm, widths[1])
    h = []
    for i in range(2):
        t = mm(q1[i], wmt)
        h.append(jnp.concatenate([mm(t[:, :r], p[2 * i]), mm(t[:, r:], p[2 * i + 1])], 1))
    top = pair(f1[0], f1[1], mmt(mm(h[0], cross), h[1]))
    _, q2 = level([mm(wmt, top)], wm, widths[2])
    t = mm(q2[0], wmt)
    last = [mm(t[:, :r], h[0]), mm(t[:, r:], h[1])]
    for w in range(4):
        out_ref[:, w * 2 * r : (w + 1) * 2 * r] = mm(last[w // 2][:, w % 2 * r : (w % 2 + 1) * r], leaf_t_ref[...])


def factors(red, leaf, merge, widths=((4, 4), (8, 8), (8, 8))):
    r = leaf.shape[1]
    return pl.pallas_call(
        functools.partial(factor_kernel, widths),
        out_shape=jax.ShapeDtypeStruct((r, 4 * leaf.shape[0]), jnp.float32),
        in_specs=[VMEM] * 5,
        out_specs=VMEM,
        compiler_params=PARAMS,
        name="factors",
    )(red, leaf, leaf.T, merge, merge.T)


def dot_rows(a, b):
    return lax.dot_general(a, b, (((1,), (1,)), ((), ())), preferred_element_type=jnp.float32)


def split(x):
    high = x.astype(jnp.bfloat16)
    return high, (x - high.astype(jnp.float32)).astype(jnp.bfloat16)


def gram_kernel(order_ref, leaf_ref, leaf_t_ref, p0, p1, p2, p3, red_ref, high_ref, low_ref):
    for d, part in enumerate((p0, p1, p2, p3)):
        per = part.shape[0] // 4
        for w in range(4):
            at = pl.ds(pl.multiple_of(w * 4 * per + order_ref[d] * per, per), per)
            high, low = split(part[w * per : (w + 1) * per, :])
            high_ref[at, :] = high
            low_ref[at, :] = low
    wl, wlt = leaf_ref[...], leaf_t_ref[...]
    k, r = wl.shape
    ha, hb = high_ref[: 2 * k, :], high_ref[2 * k :, :]
    la, lb = low_ref[: 2 * k, :], low_ref[2 * k :, :]

    def own(h, l):
        mixed = dot_rows(h, l)
        return dot_rows(h, h) + (dot_rows(l, l) + (mixed + mixed.T))

    gaa, gbb = own(ha, la), own(hb, lb)
    gab = dot_rows(ha, hb) + (dot_rows(ha, lb) + dot_rows(la, hb) + dot_rows(la, lb))
    for w, g in enumerate((gaa[:k, :k], gaa[k:, k:], gbb[:k, :k], gbb[k:, k:])):
        red_ref[w * r : (w + 1) * r, :] = mm(wlt, g)
    for at, lane, g in (
        (4, 0, gaa[:k, k:]),
        (4, 1, gbb[:k, k:]),
        (5, 0, gab[:k, :k]),
        (5, 1, gab[:k, k:]),
        (6, 0, gab[k:, :k]),
        (6, 1, gab[k:, k:]),
    ):
        red_ref[at * r : (at + 1) * r, lane * r : (lane + 1) * r] = mm(mm(wlt, g), wl)
    red_ref[7 * r :, :] = jnp.zeros((r, k), jnp.float32)


def grams(order, leaf, parts):
    k, r = leaf.shape
    cells = parts[0].shape[1]
    return pl.pallas_call(
        gram_kernel,
        out_shape=(
            jax.ShapeDtypeStruct((8 * r, k), jnp.float32),
            jax.ShapeDtypeStruct((4 * k, cells), jnp.bfloat16),
            jax.ShapeDtypeStruct((4 * k, cells), jnp.bfloat16),
        ),
        in_specs=[SMEM] + [VMEM] * 6,
        out_specs=(VMEM,) * 3,
        compiler_params=PARAMS,
        name="grams",
    )(order, leaf, leaf.T, *parts)


def modes_kernel(coef_ref, high_ref, low_ref, out_ref):
    ch, cl = split(coef_ref[...])

    def dot(a, b):
        return jnp.dot(a, b, preferred_element_type=jnp.float32)

    out_ref[...] = dot(ch, high_ref[...]) + (dot(ch, low_ref[...]) + dot(cl, high_ref[...]))


def modes(coef, high, low):
    return pl.pallas_call(
        modes_kernel,
        out_shape=jax.ShapeDtypeStruct((coef.shape[0], high.shape[1]), jnp.float32),
        in_specs=[VMEM] * 3,
        out_specs=VMEM,
        compiler_params=PARAMS,
        name="modes",
    )(coef, high, low)


def place_kernel(order_ref, p0, p1, p2, p3, out_ref):
    cells = p0.shape[1]
    for d, part in enumerate((p0, p1, p2, p3)):
        out_ref[:, pl.ds(pl.multiple_of(order_ref[d] * cells, cells), cells)] = part[...]


def place(order, parts):
    rows, cells = parts[0].shape
    return pl.pallas_call(
        place_kernel,
        out_shape=jax.ShapeDtypeStruct((rows, 4 * cells), jnp.float32),
        in_specs=[SMEM] + [VMEM] * 4,
        out_specs=VMEM,
        compiler_params=PARAMS,
        name="place",
    )(order, *parts)


def ring(axis, step):
    n = lax.axis_size(axis)
    return [(i, (i + step) % n) for i in range(n)]


def a2a(v, axis):
    return lax.all_to_all(v, axis, 0, 0, tiled=True)


def spread_over(v, axis):
    n = lax.axis_size(axis)
    return a2a(jnp.broadcast_to(v[None], (n, *v.shape)), axis)


def sum_everywhere(v):
    rows, lanes = v.shape
    core = lax.axis_index("core")
    half = v.reshape(2, rows // 2, lanes)
    mine = lax.dynamic_index_in_dim(half, core, 0, keepdims=False)
    theirs = lax.dynamic_index_in_dim(half, 1 - core, 0, keepdims=False)
    v = mine + lax.ppermute(theirs, "core", ring("core", 1))
    n = lax.axis_size("z")
    v = a2a(v.reshape(n, rows // 2 // n, lanes), "z").sum(0)
    v = spread_over(v, ("x", "tm")).sum(0)
    v = spread_over(v, "z").reshape(rows // 2, lanes)
    other = lax.ppermute(v, "core", ring("core", 1))
    return jnp.concatenate([jnp.where(core == 0, v, other), jnp.where(core == 0, other, v)], 0)


def on_device(archive, leaf_sketch, merge_sketch):
    t = lax.axis_index("tm")
    n = lax.axis_size("tm")
    k, r = leaf_sketch.shape
    cells = archive.shape[1] // n
    leaf = leaf_sketch.reshape(k // n, n, r).transpose(1, 0, 2).reshape(k, r)
    order = (t - jnp.arange(n, dtype=jnp.int32)) % n

    def chunk(d):
        return lax.dynamic_slice_in_dim(archive, (t + d) % n * cells, cells, 1)

    parts = [chunk(0)] + [None] * (n - 1)
    for d in (1, n - 1, *range(2, n - 1)):
        parts[d] = lax.ppermute(chunk(d), "tm", ring("tm", d))
    red, high, low = grams(order, leaf, parts)
    coef = factors(sum_everywhere(red), leaf, merge_sketch)
    rows = r // n
    out = modes(coef, high, low).reshape(n, rows, cells)

    def share(d):
        return lax.dynamic_index_in_dim(out, (t + d) % n, 0, keepdims=False)

    back = [share(0)] + [None] * (n - 1)
    for d in (1, n - 1, *range(2, n - 1)):
        back[d] = lax.ppermute(share(d), "tm", ring("tm", d))
    return place(order, back)


def solution(mesh):
    fine = Mesh(mesh.devices.reshape(mesh.devices.shape[0] // 8, 4, 2, 4), (*SPACE, "tm"))
    return jax.shard_map(
        on_device, mesh=fine, in_specs=(P("tm", SPACE), P(), P()), out_specs=P("tm", SPACE), check_vma=False
    )
```

```python
import functools

import jax
import jax.numpy as jnp
from jax import lax
from jax.experimental import pallas as pl
from jax.experimental.pallas import tpu as pltpu
from jax.sharding import Mesh, PartitionSpec as P

HI = lax.Precision.HIGHEST
SUB = 8
VMEM = pl.BlockSpec(memory_space=pltpu.VMEM)
ANY = pl.BlockSpec(memory_space=pl.ANY)
SPACE = ("z", "x", "core")
PARAMS = pltpu.CompilerParams(vmem_limit_bytes=56 * 2**20)
CHUNKS = (512, 512, 512, 512)
PLAN = (((16, True), (16, True)), ((8, False), (16, False)), ((16, False), (16, False)))


def mm(a, b):
    return jnp.dot(a, b, precision=HI, preferred_element_type=jnp.float32)


def mmt(a, b):
    return lax.dot_general(a, b, (((1,), (1,)), ((), ())), precision=HI, preferred_element_type=jnp.float32)


def mtm(a, b):
    return lax.dot_general(a, b, (((0,), (0,)), ((), ())), precision=HI, preferred_element_type=jnp.float32)


def eliminate(mats, width, product, packed=False):
    n, lanes = mats[0].shape
    count = n // SUB
    rows = lax.broadcasted_iota(jnp.int32, (SUB, lanes), 0)
    left = lax.broadcasted_iota(jnp.int32, (SUB, lanes), 1) < n
    work = [[m[b * SUB : (b + 1) * SUB, :] for b in range(count)] for m in mats]

    def row(v, c):
        return jnp.broadcast_to(v[c : c + 1, :], (SUB, lanes))

    def column(v, c):
        wide = jnp.broadcast_to(v[:, c : c + 1], (SUB, lanes))
        if not packed:
            return wide
        return jnp.where(left, wide, jnp.broadcast_to(v[:, n + c : n + c + 1], (SUB, lanes)))

    for first in range(0, n, width):
        lo, hi = first // SUB, (first + width + SUB - 1) // SUB
        end = hi if product else count
        spread = [
            [{b: column(w[b], first + c) for b in range((first + c) // SUB, end)} for c in range(width)] for w in work
        ]
        pivots = [[] for _ in mats]
        for c in range(width):
            p, at = divmod(first + c, SUB)
            for w, t, d in zip(work, spread, pivots):
                d.append(row(t[c][p], at))
                inverse = 1.0 / d[c]
                pivot_row = row(w[p], at) * inverse
                for later in range(c + 1, width):
                    lp, lat = divmod(first + later, SUB)
                    scale = row(t[c][lp], lat) * inverse
                    for b in range(lp, end):
                        t[later][b] = t[later][b] - t[c][b] * scale
                w[p] = w[p] - jnp.where(rows > at, t[c][p], 0.0) * pivot_row
                for b in range(p + 1, end):
                    w[b] = w[b] - t[c][b] * pivot_row
        for w, d in zip(work, pivots):
            for b in range(lo, hi):
                scale = d[(b - lo) * SUB]
                for at in range(1, SUB):
                    scale = jnp.where(rows >= at, d[(b - lo) * SUB + at], scale)
                w[b] = w[b] * lax.rsqrt(scale)
            if product and hi < count:
                top = jnp.concatenate(w[lo:hi], 0)
                if packed:
                    below = jnp.concatenate([mtm(top[:, :n], top[:, :n]), mtm(top[:, n:], top[:, n:])], 1)
                else:
                    below = mtm(top[:, :n], top)
                for b in range(hi, count):
                    w[b] = w[b] - below[b * SUB : (b + 1) * SUB, :]
    return [jnp.concatenate(w, 0) for w in work]


def factor(sketched, grams, plan):
    r = sketched[0].shape[0]
    row = lax.broadcasted_iota(jnp.int32, (r, r), 0)
    lane = lax.broadcasted_iota(jnp.int32, (r, r), 1)
    eye = (row == lane).astype(jnp.float32)
    whole = eliminate([jnp.concatenate([s, eye], 1) for s in sketched], *plan[0])
    inverse = [e[:, r:] for e in whole]
    mixed = [mm(i, b) for i, b in zip(inverse, grams)]
    inner = [mmt(m, m) for m in mixed]
    if len(inner) > 1:
        both = [jnp.concatenate(inner[i : i + 2], 1) for i in range(0, len(inner), 2)]
        both = eliminate(both, *plan[1], packed=True)
        upper = [half for e in both for half in (e[:, :r], e[:, r:])]
    else:
        upper = eliminate(inner, *plan[1])
    return inverse, [jnp.where(lane >= row, u, 0.0) for u in upper]


def stack_pair(upper, maps, cross, sketch):
    ua, ub = upper
    r = ua.shape[0]
    va, vb = mtm(sketch[:r, :], ua), mtm(sketch[r:, :], ub)
    ta, tb = va + mmt(vb, cross), vb + mm(va, cross)
    sketched = mmt(ta, va) + mmt(tb, vb)
    gram = jnp.concatenate([mmt(ta, ua), mmt(tb, ub)], 1)
    return sketched, gram, jnp.concatenate([mm(va, maps[0]), mm(vb, maps[1])], 1)


def combine(red_ref, wl, wm):
    r = wl.shape[1]
    grams = [red_ref[w * r : (w + 1) * r, :] for w in range(4)]
    z, u = factor([mm(g, wl) for g in grams], grams, PLAN[0])
    pairs = []
    for i in range(2):
        cross = mmt(mm(z[2 * i], red_ref[4 * r : 5 * r, i * r : (i + 1) * r]), z[2 * i + 1])
        pairs.append(stack_pair(u[2 * i : 2 * i + 2], z[2 * i : 2 * i + 2], cross, wm))
    inverse, u = factor([p[0] for p in pairs], [p[1] for p in pairs], PLAN[1])
    z = [mm(i, p[2]) for i, p in zip(inverse, pairs)]
    cross = mmt(mm(z[0], red_ref[5 * r : 7 * r, :]), z[1])
    sketched, gram, rows = stack_pair(u, z, cross, wm)
    inverse, u = factor([sketched], [gram], PLAN[2])
    z = mm(inverse[0], rows)
    return u[0], jnp.concatenate([mmt(z[:, w * r : (w + 1) * r], wl) for w in range(4)], 1)


def dot_rows(a, b):
    return lax.dot_general(a, b, (((1,), (1,)), ((), ())), preferred_element_type=jnp.float32)


def split(x):
    high = x.astype(jnp.bfloat16)
    return high, (x - high.astype(jnp.float32)).astype(jnp.bfloat16)


def in_window_order(leaf_ref):
    k = leaf_ref.shape[0]
    return jnp.concatenate([leaf_ref[pl.ds(j, k // 4, stride=4), :] for j in range(4)], 0)


def cut_kernel(base, archive_ref, o1, o2, o3, sem):
    t = lax.axis_index("tm")
    cells = archive_ref.shape[1] // 4
    copies = []
    for d, out in enumerate((o1, o2, o3)):
        at = pl.multiple_of(lax.rem(t + d + 1, 4) * cells + base, 128)
        copies.append(pltpu.make_async_copy(archive_ref.at[:, pl.ds(at, out.shape[1])], out, sem.at[d]))
    for copy in copies:
        copy.start()
    for copy in copies:
        copy.wait()


def cut(archive, base, step):
    return pl.pallas_call(
        functools.partial(cut_kernel, base),
        out_shape=(jax.ShapeDtypeStruct((archive.shape[0], step), jnp.float32),) * 3,
        in_specs=[ANY],
        out_specs=(ANY,) * 3,
        scratch_shapes=[pltpu.SemaphoreType.DMA((3,))],
        compiler_params=PARAMS,
        name="cut",
    )(archive)


def gram_kernel(base, first, last, leaf_ref, archive_ref, p1, p2, p3, *refs):
    sofar, refs = refs[: not first], refs[not first :]
    sums, (high_out, low_out, held, high_ref, low_ref, red, sem) = refs[: 1 + last], refs[1 + last :]
    t = lax.axis_index("tm")
    step = held.shape[2]
    mine = pl.multiple_of(t * (archive_ref.shape[1] // 4) + base, 128)
    sources = (archive_ref.at[:, pl.ds(mine, step)], p1, p2, p3)
    copies = [pltpu.make_async_copy(p, held.at[d], sem.at[d]) for d, p in enumerate(sources)]
    for copy in copies:
        copy.start()
    for d, copy in enumerate(copies):
        copy.wait()
        per = held.shape[1] // 4
        for w in range(4):
            at = pl.ds(pl.multiple_of(w * 4 * per + lax.rem(t + 4 - d, 4) * per, per), per)
            high, low = split(held[d, w * per : (w + 1) * per, :])
            high_ref[at, :] = high
            low_ref[at, :] = low
    outward = [pltpu.make_async_copy(high_ref, high_out, sem.at[4]), pltpu.make_async_copy(low_ref, low_out, sem.at[5])]
    for copy in outward:
        copy.start()
    k, r = leaf_ref.shape
    halves = [(ref[: 2 * k, :], ref[2 * k :, :]) for ref in (high_ref, low_ref)]

    def block(index, i, j):
        hi, li, hj, lj = halves[0][i], halves[1][i], halves[0][j], halves[1][j]
        g = dot_rows(hi, hj) + (dot_rows(hi, lj) + dot_rows(li, hj) + dot_rows(li, lj))
        return g if first else sofar[0][index * 2 * k : (index + 1) * 2 * k, :] + g

    blocks = [block(index, i, j) for index, (i, j) in enumerate(((0, 0), (1, 1), (0, 1)))]
    if last:
        wl = in_window_order(leaf_ref)
        blank = jnp.zeros_like(wl)
        wide = jnp.concatenate([jnp.concatenate([wl, blank], 1), jnp.concatenate([blank, wl], 1)], 0)
        own = [mtm(wide, g) for g in blocks]
        for w in range(4):
            red[w * r : (w + 1) * r, :] = own[w // 2][w % 2 * r : (w % 2 + 1) * r, w % 2 * k : (w % 2 + 1) * k]
        beside = mm(jnp.concatenate([own[0][:r, k:], own[1][:r, k:]], 0), wl)
        red[4 * r : 5 * r, :] = jnp.concatenate([beside[:r], beside[r:]], 1)
        red[5 * r : 7 * r, :] = mm(own[2], wide)
        red[7 * r :, :] = jnp.zeros((r, k), jnp.float32)
        core = lax.axis_index("core")
        half = 4 * r
        sums[0][...] = red[pl.ds(pl.multiple_of(core * half, half), half), :]
        sums[1][...] = red[pl.ds(pl.multiple_of((1 - core) * half, half), half), :]
    else:
        for index, g in enumerate(blocks):
            sums[0][index * 2 * k : (index + 1) * 2 * k, :] = g
    for copy in outward:
        copy.wait()


def grams(base, leaf, archive, parts, sofar, last):
    k, r = leaf.shape
    rows, step = parts[0].shape
    halves = (jax.ShapeDtypeStruct((4 * k, step), jnp.bfloat16),) * 2
    if last:
        sums = (jax.ShapeDtypeStruct((4 * r, k), jnp.float32),) * 2
    else:
        sums = (jax.ShapeDtypeStruct((6 * k, 2 * k), jnp.float32),)
    return pl.pallas_call(
        functools.partial(gram_kernel, base, not sofar, last),
        out_shape=sums + halves,
        in_specs=[VMEM] + [ANY] * 4 + [VMEM] * len(sofar),
        out_specs=(VMEM,) * len(sums) + (ANY,) * 2,
        scratch_shapes=[
            pltpu.VMEM((4, rows, step), jnp.float32),
            pltpu.VMEM((4 * k, step), jnp.bfloat16),
            pltpu.VMEM((4 * k, step), jnp.bfloat16),
            pltpu.VMEM((8 * r, k), jnp.float32),
            pltpu.SemaphoreType.DMA((6,)),
        ],
        compiler_params=PARAMS,
        name="grams",
    )(leaf, archive, *parts, *sofar)


def modes_kernel(count, mine_ref, other_ref, leaf_ref, merge_ref, *refs):
    sources, outs, (red, held, total, sem) = refs[: 2 * count], refs[2 * count : -4], refs[-4:]
    copies, at = [], [0, 0]
    for i, s in enumerate(sources):
        side = i // count
        copies.append(pltpu.make_async_copy(s, held.at[side, :, pl.ds(at[side], s.shape[1])], sem.at[i]))
        at[side] += s.shape[1]
    for copy in copies:
        copy.start()
    core = lax.axis_index("core")
    half = mine_ref.shape[0]
    red[pl.ds(pl.multiple_of(core * half, half), half), :] = mine_ref[...]
    red[pl.ds(pl.multiple_of((1 - core) * half, half), half), :] = other_ref[...]
    scale, rows = combine(red, in_window_order(leaf_ref), merge_ref[...])
    high, low = split(rows)

    def dot(a, b):
        return jnp.dot(a, b, preferred_element_type=jnp.float32)

    for copy in copies:
        copy.wait()
    basis = dot(high, held[0]) + (dot(high, held[1]) + dot(low, held[0]))
    total[...] = mm(scale, basis)
    t = lax.axis_index("tm")
    per = outs[0].shape[0]
    for d, out in enumerate(outs):
        out[...] = total[pl.ds(pl.multiple_of(lax.rem(t + d, 4) * per, per), per), :]


def modes(mine, other, leaf, merge, high, low):
    k, r = leaf.shape
    count, cells = len(high), sum(h.shape[1] for h in high)
    return pl.pallas_call(
        functools.partial(modes_kernel, count),
        out_shape=(jax.ShapeDtypeStruct((r // 4, cells), jnp.float32),) * 4,
        in_specs=[VMEM] * 4 + [ANY] * (2 * count),
        out_specs=(VMEM,) * 4,
        scratch_shapes=[
            pltpu.VMEM((8 * r, k), jnp.float32),
            pltpu.VMEM((2, 4 * k, cells), jnp.bfloat16),
            pltpu.VMEM((r, cells), jnp.float32),
            pltpu.SemaphoreType.DMA((2 * count,)),
        ],
        compiler_params=PARAMS,
        name="modes",
    )(mine, other, leaf, merge, *high, *low)


def ring(axis, step):
    n = lax.axis_size(axis)
    return [(i, (i + step) % n) for i in range(n)]


def a2a(v, axis):
    return lax.all_to_all(v, axis, 0, 0, tiled=True)


def spread_over(v, axis):
    n = lax.axis_size(axis)
    return a2a(jnp.broadcast_to(v[None], (n, *v.shape)), axis)


def sum_everywhere(mine, theirs):
    rows, lanes = mine.shape
    n = lax.axis_size("z")
    v = mine + lax.ppermute(theirs, "core", ring("core", 1))
    v = a2a(v.reshape(n, rows // n, lanes), "z").sum(0)
    v = spread_over(v, ("x", "tm")).sum(0)
    v = spread_over(v, "z").reshape(rows, lanes)
    return v, lax.ppermute(v, "core", ring("core", 1))


def on_device(archive, leaf, merge):
    r = leaf.shape[1]
    n = lax.axis_size("tm")
    t = lax.axis_index("tm")
    cells = archive.shape[1] // n
    sends = (2, 1, 3)
    bases = [sum(CHUNKS[:c]) for c in range(len(CHUNKS))]
    moved = []
    for base, step in zip(bases, CHUNKS):
        pieces = cut(archive, base, step)
        moved.append({d: lax.ppermute(pieces[d - 1], "tm", ring("tm", d)) for d in sends})
    sums, high, low = [], [], []
    for c, (base, parts) in enumerate(zip(bases, moved)):
        *sums, h, l = grams(base, leaf, archive, [parts[d] for d in (1, 2, 3)], sums, c == len(CHUNKS) - 1)
        high.append(h)
        low.append(l)
    out = modes(*sum_everywhere(*sums), leaf, merge, high, low)
    back = {d: lax.ppermute(out[d], "tm", ring("tm", d)) for d in sends}
    whole = lax.dynamic_update_slice_in_dim(jnp.zeros((r // n, n * cells), jnp.float32), out[0], t * cells, 1)
    for d in sends:
        whole = lax.dynamic_update_slice_in_dim(whole, back[d], (t + n - d) % n * cells, 1)
    return whole


def solution(mesh):
    fine = Mesh(mesh.devices.reshape(mesh.devices.shape[0] // 8, 4, 2, 4), (*SPACE, "tm"))
    return jax.shard_map(
        on_device, mesh=fine, in_specs=(P("tm", SPACE), P(), P()), out_specs=P("tm", SPACE), check_vma=False
    )
```

```python
import functools

import jax
import jax.numpy as jnp
from jax import lax
from jax.experimental import pallas as pl
from jax.experimental.pallas import tpu as pltpu
from jax.sharding import Mesh, PartitionSpec as P

HI = lax.Precision.HIGHEST
SUB = 8
VMEM = pl.BlockSpec(memory_space=pltpu.VMEM)
ANY = pl.BlockSpec(memory_space=pl.ANY)
in_space = pltpu.with_memory_space_constraint
SPACE = ("z", "x", "core")
PARAMS = pltpu.CompilerParams(vmem_limit_bytes=12 * 2**20)
CHUNKS = (512, 512, 640, 384)
PLAN = (((16, True), (16, True)), ((8, False), (16, False)), ((16, False), (16, False)))


def mm(a, b):
    return jnp.dot(a, b, precision=HI, preferred_element_type=jnp.float32)


def mmt(a, b):
    return lax.dot_general(a, b, (((1,), (1,)), ((), ())), precision=HI, preferred_element_type=jnp.float32)


def mtm(a, b):
    return lax.dot_general(a, b, (((0,), (0,)), ((), ())), precision=HI, preferred_element_type=jnp.float32)


def eliminate(mats, width, product, packed=False):
    n, lanes = mats[0].shape
    count = n // SUB
    rows = lax.broadcasted_iota(jnp.int32, (SUB, lanes), 0)
    left = lax.broadcasted_iota(jnp.int32, (SUB, lanes), 1) < n
    work = [[m[b * SUB : (b + 1) * SUB, :] for b in range(count)] for m in mats]

    def row(v, c):
        return jnp.broadcast_to(v[c : c + 1, :], (SUB, lanes))

    def column(v, c):
        wide = jnp.broadcast_to(v[:, c : c + 1], (SUB, lanes))
        if not packed:
            return wide
        return jnp.where(left, wide, jnp.broadcast_to(v[:, n + c : n + c + 1], (SUB, lanes)))

    for first in range(0, n, width):
        lo, hi = first // SUB, (first + width + SUB - 1) // SUB
        end = hi if product else count
        spread = [
            [{b: column(w[b], first + c) for b in range((first + c) // SUB, end)} for c in range(width)] for w in work
        ]
        pivots = [[] for _ in mats]
        for c in range(width):
            p, at = divmod(first + c, SUB)
            for w, t, d in zip(work, spread, pivots):
                d.append(row(t[c][p], at))
                inverse = 1.0 / d[c]
                pivot_row = row(w[p], at) * inverse
                for later in range(c + 1, width):
                    lp, lat = divmod(first + later, SUB)
                    scale = row(t[c][lp], lat) * inverse
                    for b in range(lp, end):
                        t[later][b] = t[later][b] - t[c][b] * scale
                w[p] = w[p] - jnp.where(rows > at, t[c][p], 0.0) * pivot_row
                for b in range(p + 1, end):
                    w[b] = w[b] - t[c][b] * pivot_row
        for w, d in zip(work, pivots):
            for b in range(lo, hi):
                scale = d[(b - lo) * SUB]
                for at in range(1, SUB):
                    scale = jnp.where(rows >= at, d[(b - lo) * SUB + at], scale)
                w[b] = w[b] * lax.rsqrt(scale)
            if product and hi < count:
                top = jnp.concatenate(w[lo:hi], 0)
                if packed:
                    below = jnp.concatenate([mtm(top[:, :n], top[:, :n]), mtm(top[:, n:], top[:, n:])], 1)
                else:
                    below = mtm(top[:, :n], top)
                for b in range(hi, count):
                    w[b] = w[b] - below[b * SUB : (b + 1) * SUB, :]
    return [jnp.concatenate(w, 0) for w in work]


def factor(sketched, grams, plan):
    r = sketched[0].shape[0]
    row = lax.broadcasted_iota(jnp.int32, (r, r), 0)
    lane = lax.broadcasted_iota(jnp.int32, (r, r), 1)
    eye = (row == lane).astype(jnp.float32)
    whole = eliminate([jnp.concatenate([s, eye], 1) for s in sketched], *plan[0])
    inverse = [e[:, r:] for e in whole]
    mixed = [mm(i, b) for i, b in zip(inverse, grams)]
    inner = [mmt(m, m) for m in mixed]
    if len(inner) > 1:
        both = [jnp.concatenate(inner[i : i + 2], 1) for i in range(0, len(inner), 2)]
        both = eliminate(both, *plan[1], packed=True)
        upper = [half for e in both for half in (e[:, :r], e[:, r:])]
    else:
        upper = eliminate(inner, *plan[1])
    return inverse, [jnp.where(lane >= row, u, 0.0) for u in upper]


def stack_pair(upper, maps, cross, sketch_t):
    ua, ub = upper
    r = ua.shape[0]
    va, vb = mm(sketch_t[:, :r], ua), mm(sketch_t[:, r:], ub)
    ta, tb = va + mmt(vb, cross), vb + mm(va, cross)
    sketched = mmt(ta, va) + mmt(tb, vb)
    gram = jnp.concatenate([mmt(ta, ua), mmt(tb, ub)], 1)
    return sketched, gram, jnp.concatenate([mm(va, maps[0]), mm(vb, maps[1])], 1)


def combine(red_ref, wl, wmt):
    r = wl.shape[1]
    grams = [red_ref[w * r : (w + 1) * r, :] for w in range(4)]
    z, u = factor([mm(g, wl) for g in grams], grams, PLAN[0])
    pairs = []
    for i in range(2):
        cross = mmt(mm(z[2 * i], red_ref[4 * r : 5 * r, i * r : (i + 1) * r]), z[2 * i + 1])
        pairs.append(stack_pair(u[2 * i : 2 * i + 2], z[2 * i : 2 * i + 2], cross, wmt))
    inverse, u = factor([p[0] for p in pairs], [p[1] for p in pairs], PLAN[1])
    z = [mm(i, p[2]) for i, p in zip(inverse, pairs)]
    cross = mmt(mm(z[0], red_ref[5 * r : 7 * r, :]), z[1])
    sketched, gram, rows = stack_pair(u, z, cross, wmt)
    inverse, u = factor([sketched], [gram], PLAN[2])
    z = mm(inverse[0], rows)
    return u[0], jnp.concatenate([mmt(z[:, w * r : (w + 1) * r], wl) for w in range(4)], 1)


def dot_rows(a, b):
    return lax.dot_general(a, b, (((1,), (1,)), ((), ())), preferred_element_type=jnp.float32)


def split(x):
    high = x.astype(jnp.bfloat16)
    return high, (x - high.astype(jnp.float32)).astype(jnp.bfloat16)


def store_halves(t, d, rows_ref, high_ref, low_ref):
    per = rows_ref.shape[0] // 4
    for w in range(4):
        at = pl.ds(pl.multiple_of(w * 4 * per + lax.rem(t + 4 - d, 4) * per, per), per)
        high_ref[at, :], low_ref[at, :] = split(rows_ref[w * per : (w + 1) * per, :])


def own_cells(archive_ref, t, base, step):
    at = pl.multiple_of(t * (archive_ref.shape[1] // 4) + base, 128)
    return archive_ref.at[:, pl.ds(at, step)]


def gram_kernel(base, first, last, sketch_ref, archive_ref, p1, p2, p3, *refs):
    sofar, refs = refs[: not first], refs[not first :]
    sums, refs = refs[: 1 + last], refs[1 + last :]
    (high_ref, low_ref), refs = refs[:2], refs[2:]
    sketch_out, (held, red, sem, *turned) = refs[:first], refs[first:]
    t = lax.axis_index("tm")
    step = held.shape[2]
    sources = (own_cells(archive_ref, t, base, step), p1, p2, p3)
    copies = [pltpu.make_async_copy(p, held.at[d], sem.at[d]) for d, p in enumerate(sources)]
    for copy in copies:
        copy.start()
    if first:
        k = sketch_ref.shape[1]
        turned[0][...] = sketch_ref[...].T
        wl = jnp.concatenate([turned[0][pl.ds(j, k // 4, stride=4), :] for j in range(4)], 0)
        sketch_out[0][...] = wl
    else:
        wl = sketch_ref[...]
    k, r = wl.shape
    for d, copy in enumerate(copies):
        copy.wait()
        store_halves(t, d, held.at[d], high_ref, low_ref)
    halves = [(ref[: 2 * k, :], ref[2 * k :, :]) for ref in (high_ref, low_ref)]

    def block(i, j):
        hi, li, hj, lj = halves[0][i], halves[1][i], halves[0][j], halves[1][j]
        return dot_rows(hi, hj) + (dot_rows(hi, lj) + dot_rows(li, hj) + dot_rows(li, lj))

    blank = jnp.zeros_like(wl)
    wide = jnp.concatenate([jnp.concatenate([wl, blank], 1), jnp.concatenate([blank, wl], 1)], 0)
    own = [mtm(wide, block(i, j)) for i, j in ((0, 0), (1, 1), (0, 1))]

    def add(at, value):
        to = slice(at * r, at * r + value.shape[0])
        red[to, :] = value if first else sofar[0][to, :] + value

    for w in range(4):
        add(w, own[w // 2][w % 2 * r : (w % 2 + 1) * r, w % 2 * k : (w % 2 + 1) * k])
    beside = mm(jnp.concatenate([own[0][:r, k:], own[1][:r, k:]], 0), wl)
    add(4, jnp.concatenate([beside[:r], beside[r:]], 1))
    add(5, mm(own[2], wide))
    if first:
        red[7 * r :, :] = jnp.zeros((r, k), jnp.float32)
    else:
        red[7 * r :, :] = sofar[0][7 * r :, :]
    if last:
        core = lax.axis_index("core")
        half = 4 * r
        sums[0][...] = red[pl.ds(pl.multiple_of(core * half, half), half), :]
        sums[1][...] = red[pl.ds(pl.multiple_of((1 - core) * half, half), half), :]
    else:
        sums[0][...] = red[...]


def grams(base, sketch, archive, parts, sofar, last):
    first = not sofar
    k, r = max(sketch.shape), min(sketch.shape)
    rows, step = parts[0].shape
    halves = ((jax.ShapeDtypeStruct if first else pltpu.VMEM)((4 * k, step), jnp.bfloat16),) * 2
    sums = (jax.ShapeDtypeStruct((4 * r if last else 8 * r, k), jnp.float32),) * (1 + last)
    ordered = (jax.ShapeDtypeStruct((k, r), jnp.float32),) * first
    return pl.pallas_call(
        functools.partial(gram_kernel, base, first, last),
        out_shape=sums + halves + ordered,
        in_specs=[VMEM] + [ANY] * 4 + [VMEM] * len(sofar),
        out_specs=(VMEM,) * (len(sums) + 2 + first),
        scratch_shapes=[
            pltpu.VMEM((4, rows, step), jnp.float32),
            pltpu.VMEM((8 * r, k), jnp.float32),
            pltpu.SemaphoreType.DMA((4,)),
        ]
        + [pltpu.VMEM((k, r), jnp.float32)] * first,
        compiler_params=PARAMS,
        cost_estimate=pl.CostEstimate(flops=128 * k * k * step, bytes_accessed=48 * k * step, transcendentals=0),
        name="grams",
    )(sketch, in_space(archive, pltpu.HBM), *parts, *sofar)


def modes_kernel(count, mine_ref, other_ref, leaf_ref, merge_ref, *refs):
    highs, lows, outs, (red, total, early, sem) = refs[:count], refs[count : 2 * count], refs[2 * count : -4], refs[-4:]
    fetches = [pltpu.make_async_copy(s[0], early.at[i], sem.at[i]) for i, s in enumerate((highs, lows))]
    for fetch in fetches:
        fetch.start()
    t = lax.axis_index("tm")
    core = lax.axis_index("core")
    half = mine_ref.shape[0]
    red[pl.ds(pl.multiple_of(core * half, half), half), :] = mine_ref[...]
    red[pl.ds(pl.multiple_of((1 - core) * half, half), half), :] = other_ref[...]
    a, b = split(mm(*combine(red, leaf_ref[...], merge_ref[...])))

    def dot(a, b):
        return jnp.dot(a, b, preferred_element_type=jnp.float32)

    for fetch in fetches:
        fetch.wait()
    at = 0
    for high, low in zip((early.at[0], *highs[1:]), (early.at[1], *lows[1:])):
        step = high.shape[1]
        total[:, at : at + step] = dot(a, high[...]) + (dot(a, low[...]) + dot(b, high[...]))
        at += step
    per = outs[0].shape[0]
    for d, out in enumerate(outs):
        out[...] = total[pl.ds(pl.multiple_of(lax.rem(t + d, 4) * per, per), per), :]


def modes(mine, other, leaf, merge, high, low):
    k, r = leaf.shape
    count, cells = len(high), sum(h.shape[1] for h in high)
    return pl.pallas_call(
        functools.partial(modes_kernel, count),
        out_shape=(jax.ShapeDtypeStruct((r // 4, cells), jnp.float32),) * 4,
        in_specs=[VMEM] * 4 + ([ANY] + [VMEM] * (count - 1)) * 2,
        out_specs=(VMEM,) * 4,
        scratch_shapes=[
            pltpu.VMEM((8 * r, k), jnp.float32),
            pltpu.VMEM((r, cells), jnp.float32),
            pltpu.VMEM((2, *high[0].shape), jnp.bfloat16),
            pltpu.SemaphoreType.DMA((2,)),
        ],
        compiler_params=PARAMS,
        name="modes",
    )(mine, other, leaf, merge, *(in_space(v, pltpu.VMEM if i else pltpu.HBM) for s in (high, low) for i, v in enumerate(s)))


def place_kernel(p0, p1, p2, p3, out_ref, sem):
    t = lax.axis_index("tm")
    cells = p0.shape[1]
    copies = []
    for d, part in enumerate((p0, p1, p2, p3)):
        at = pl.multiple_of(lax.rem(t + 4 - d, 4) * cells, cells)
        copies.append(pltpu.make_async_copy(part, out_ref.at[:, pl.ds(at, cells)], sem.at[d]))
    for copy in copies:
        copy.start()
    for copy in copies:
        copy.wait()


def place(parts):
    rows, cells = parts[0].shape
    return pl.pallas_call(
        place_kernel,
        out_shape=jax.ShapeDtypeStruct((rows, 4 * cells), jnp.float32),
        in_specs=[ANY] * 4,
        out_specs=ANY,
        scratch_shapes=[pltpu.SemaphoreType.DMA((4,))],
        compiler_params=PARAMS,
        name="place",
    )(*parts)


def ring(axis, step):
    n = lax.axis_size(axis)
    return [(i, (i + step) % n) for i in range(n)]


def a2a(v, axis):
    return lax.all_to_all(v, axis, 0, 0, tiled=True)


def spread_over(v, axis):
    n = lax.axis_size(axis)
    return a2a(jnp.broadcast_to(v[None], (n, *v.shape)), axis)


def sum_everywhere(mine, theirs):
    rows, lanes = mine.shape
    n = lax.axis_size("z")
    v = mine + lax.ppermute(theirs, "core", ring("core", 1))
    v = a2a(v.reshape(n, rows // n, lanes), "z").sum(0)
    v = spread_over(v, ("x", "tm")).sum(0)
    v = spread_over(v, "z").reshape(rows, lanes)
    return v, lax.ppermute(v, "core", ring("core", 1))


def on_device(archive, leaf, merge):
    r = leaf.shape[1]
    n = lax.axis_size("tm")
    t = lax.axis_index("tm")
    cells = archive.shape[1] // n
    sends = (2, 1, 3)
    bases = [sum(CHUNKS[:c]) for c in range(len(CHUNKS))]
    last = len(CHUNKS) - 1

    def send(c, source):
        at = [(t + d) % n * cells + bases[c] for d in sends]
        pieces = [lax.dynamic_slice_in_dim(source, a, CHUNKS[c], 1) for a in at]
        arrived = {d: lax.ppermute(p, "tm", ring("tm", d)) for d, p in zip(sends, pieces)}
        return [arrived[d] for d in (1, 2, 3)]

    source = archive
    moved = [send(0, source)]
    source, marker = lax.optimization_barrier((source, leaf))
    moved.append(send(1, source))
    sums, high, low, sketch = [], [], [], marker.T
    for c in range(last):
        if c + 2 <= last:
            source, *moved[c] = lax.optimization_barrier((source, *moved[c]))
            moved.append(send(c + 2, source))
        if c == 0:
            total, h, l, sketch = grams(bases[c], sketch, archive, moved[c], sums, False)
        else:
            total, h, l = grams(bases[c], sketch, archive, moved[c], sums, False)
        source, total = lax.optimization_barrier((source, total))
        sums = [total]
        high.append(h)
        low.append(l)
    *sums, h, l = grams(bases[last], sketch, archive, moved[last], sums, True)
    out = modes(*sum_everywhere(*sums), sketch, merge.T, [*high, h], [*low, l])
    back = {d: lax.ppermute(out[d], "tm", ring("tm", d)) for d in sends}
    return place([out[0], *(back[d] for d in (1, 2, 3))])


def solution(mesh):
    fine = Mesh(mesh.devices.reshape(mesh.devices.shape[0] // 8, 4, 2, 4), (*SPACE, "tm"))
    return jax.shard_map(
        on_device, mesh=fine, in_specs=(P("tm", SPACE), P(), P()), out_specs=P("tm", SPACE), check_vma=False
    )
```

```python
import functools

import jax
import jax.numpy as jnp
from jax import lax
from jax.experimental import pallas as pl
from jax.experimental.pallas import tpu as pltpu
from jax.sharding import Mesh, PartitionSpec as P

HI = lax.Precision.HIGHEST
SUB = 8
VMEM = pl.BlockSpec(memory_space=pltpu.VMEM)
ANY = pl.BlockSpec(memory_space=pl.ANY)
in_space = pltpu.with_memory_space_constraint
SPACE = ("z", "x", "core")
PARAMS = pltpu.CompilerParams(vmem_limit_bytes=12 * 2**20)
CHUNKS = (512, 512, 768, 256)
PLAN = (((16, True), (16, True)), ((8, False), (16, False)), ((16, False), (16, False)))


def mm(a, b):
    return jnp.dot(a, b, precision=HI, preferred_element_type=jnp.float32)


def mmt(a, b):
    return lax.dot_general(a, b, (((1,), (1,)), ((), ())), precision=HI, preferred_element_type=jnp.float32)


def mtm(a, b):
    return lax.dot_general(a, b, (((0,), (0,)), ((), ())), precision=HI, preferred_element_type=jnp.float32)


def eliminate(mats, width, product, packed=False):
    n, lanes = mats[0].shape
    count = n // SUB
    rows = lax.broadcasted_iota(jnp.int32, (SUB, lanes), 0)
    left = lax.broadcasted_iota(jnp.int32, (SUB, lanes), 1) < n
    work = [[m[b * SUB : (b + 1) * SUB, :] for b in range(count)] for m in mats]

    def row(v, c):
        return jnp.broadcast_to(v[c : c + 1, :], (SUB, lanes))

    def column(v, c):
        wide = jnp.broadcast_to(v[:, c : c + 1], (SUB, lanes))
        if not packed:
            return wide
        return jnp.where(left, wide, jnp.broadcast_to(v[:, n + c : n + c + 1], (SUB, lanes)))

    for first in range(0, n, width):
        lo, hi = first // SUB, (first + width + SUB - 1) // SUB
        end = hi if product else count
        spread = [
            [{b: column(w[b], first + c) for b in range((first + c) // SUB, end)} for c in range(width)] for w in work
        ]
        pivots = [[] for _ in mats]
        for c in range(width):
            p, at = divmod(first + c, SUB)
            for w, t, d in zip(work, spread, pivots):
                d.append(row(t[c][p], at))
                inverse = 1.0 / d[c]
                pivot_row = row(w[p], at) * inverse
                for later in range(c + 1, width):
                    lp, lat = divmod(first + later, SUB)
                    scale = row(t[c][lp], lat) * inverse
                    for b in range(lp, end):
                        t[later][b] = t[later][b] - t[c][b] * scale
                w[p] = w[p] - jnp.where(rows > at, t[c][p], 0.0) * pivot_row
                for b in range(p + 1, end):
                    w[b] = w[b] - t[c][b] * pivot_row
        for w, d in zip(work, pivots):
            for b in range(lo, hi):
                scale = d[(b - lo) * SUB]
                for at in range(1, SUB):
                    scale = jnp.where(rows >= at, d[(b - lo) * SUB + at], scale)
                w[b] = w[b] * lax.rsqrt(scale)
            if product and hi < count:
                top = jnp.concatenate(w[lo:hi], 0)
                if packed:
                    below = jnp.concatenate([mtm(top[:, :n], top[:, :n]), mtm(top[:, n:], top[:, n:])], 1)
                else:
                    below = mtm(top[:, :n], top)
                for b in range(hi, count):
                    w[b] = w[b] - below[b * SUB : (b + 1) * SUB, :]
    return [jnp.concatenate(w, 0) for w in work]


def factor(sketched, grams, plan):
    r = sketched[0].shape[0]
    row = lax.broadcasted_iota(jnp.int32, (r, r), 0)
    lane = lax.broadcasted_iota(jnp.int32, (r, r), 1)
    eye = (row == lane).astype(jnp.float32)
    whole = eliminate([jnp.concatenate([s, eye], 1) for s in sketched], *plan[0])
    inverse = [e[:, r:] for e in whole]
    mixed = [mm(i, b) for i, b in zip(inverse, grams)]
    inner = [mmt(m, m) for m in mixed]
    if len(inner) > 1:
        both = [jnp.concatenate(inner[i : i + 2], 1) for i in range(0, len(inner), 2)]
        both = eliminate(both, *plan[1], packed=True)
        upper = [half for e in both for half in (e[:, :r], e[:, r:])]
    else:
        upper = eliminate(inner, *plan[1])
    return inverse, [jnp.where(lane >= row, u, 0.0) for u in upper]


def stack_pair(upper, maps, cross, sketch_t):
    ua, ub = upper
    r = ua.shape[0]
    va, vb = mm(sketch_t[:, :r], ua), mm(sketch_t[:, r:], ub)
    ta, tb = va + mmt(vb, cross), vb + mm(va, cross)
    sketched = mmt(ta, va) + mmt(tb, vb)
    gram = jnp.concatenate([mmt(ta, ua), mmt(tb, ub)], 1)
    return sketched, gram, jnp.concatenate([mm(va, maps[0]), mm(vb, maps[1])], 1)


def combine(red_ref, wl, wmt):
    r = wl.shape[1]
    grams = [red_ref[w * r : (w + 1) * r, :] for w in range(4)]
    z, u = factor([mm(g, wl) for g in grams], grams, PLAN[0])
    pairs = []
    for i in range(2):
        cross = mmt(mm(z[2 * i], red_ref[4 * r : 5 * r, i * r : (i + 1) * r]), z[2 * i + 1])
        pairs.append(stack_pair(u[2 * i : 2 * i + 2], z[2 * i : 2 * i + 2], cross, wmt))
    inverse, u = factor([p[0] for p in pairs], [p[1] for p in pairs], PLAN[1])
    z = [mm(i, p[2]) for i, p in zip(inverse, pairs)]
    cross = mmt(mm(z[0], red_ref[5 * r : 7 * r, :]), z[1])
    sketched, gram, rows = stack_pair(u, z, cross, wmt)
    inverse, u = factor([sketched], [gram], PLAN[2])
    z = mm(inverse[0], rows)
    return u[0], jnp.concatenate([mmt(z[:, w * r : (w + 1) * r], wl) for w in range(4)], 1)


def dot_rows(a, b):
    return lax.dot_general(a, b, (((1,), (1,)), ((), ())), preferred_element_type=jnp.float32)


def split(x):
    high = x.astype(jnp.bfloat16)
    return high, (x - high.astype(jnp.float32)).astype(jnp.bfloat16)


def store_halves(t, d, rows_ref, high_ref, low_ref):
    per = rows_ref.shape[0] // 4
    for w in range(4):
        at = pl.ds(pl.multiple_of(w * 4 * per + lax.rem(t + 4 - d, 4) * per, per), per)
        high_ref[at, :], low_ref[at, :] = split(rows_ref[w * per : (w + 1) * per, :])


def own_cells(archive_ref, t, base, step):
    at = pl.multiple_of(t * (archive_ref.shape[1] // 4) + base, 128)
    return archive_ref.at[:, pl.ds(at, step)]


def gram_kernel(base, first, last, sketch_ref, archive_ref, p1, p2, p3, *refs):
    sofar, refs = refs[: not first], refs[not first :]
    sums, refs = refs[: 1 + last], refs[1 + last :]
    halves_out, refs = refs[:2], refs[2:]
    sketch_out, (held, red, sem, *extra) = refs[:first], refs[first:]
    high_ref, low_ref = extra[:2] if first else halves_out
    t = lax.axis_index("tm")
    step = held.shape[2]
    sources = (own_cells(archive_ref, t, base, step), p1, p2, p3)
    copies = [pltpu.make_async_copy(p, held.at[d], sem.at[d]) for d, p in enumerate(sources)]
    for copy in copies:
        copy.start()
    if first:
        k = sketch_ref.shape[1]
        extra[2][...] = sketch_ref[...].T
        wl = jnp.concatenate([extra[2][pl.ds(j, k // 4, stride=4), :] for j in range(4)], 0)
        sketch_out[0][...] = wl
    else:
        wl = sketch_ref[...]
    k, r = wl.shape
    for d, copy in enumerate(copies):
        copy.wait()
        store_halves(t, d, held.at[d], high_ref, low_ref)
    outward = [pltpu.make_async_copy(a, b, sem.at[4 + i]) for i, (a, b) in enumerate(zip(extra[:2], halves_out))]
    for copy in outward:
        copy.start()
    halves = [(ref[: 2 * k, :], ref[2 * k :, :]) for ref in (high_ref, low_ref)]

    def block(i, j):
        hi, li, hj, lj = halves[0][i], halves[1][i], halves[0][j], halves[1][j]
        return dot_rows(hi, hj) + (dot_rows(hi, lj) + dot_rows(li, hj) + dot_rows(li, lj))

    blank = jnp.zeros_like(wl)
    wide = jnp.concatenate([jnp.concatenate([wl, blank], 1), jnp.concatenate([blank, wl], 1)], 0)
    sketched = mm(jnp.concatenate([block(0, 0), block(1, 1), block(0, 1)], 0), wide)
    near = lax.broadcasted_iota(jnp.int32, (k, 2 * r), 1) < r

    def add(at, value):
        to = slice(at * r, at * r + value.shape[0])
        red[to, :] = value if first else sofar[0][to, :] + value

    beside = []
    for i in range(2):
        top, bottom = sketched[2 * i * k : (2 * i + 1) * k], sketched[(2 * i + 1) * k : (2 * i + 2) * k]
        add(2 * i, jnp.where(near, top, bottom).T)
        beside.append(top[:, r:])
    add(4, mtm(wl, jnp.concatenate(beside, 1)))
    add(5, mtm(wide, sketched[4 * k :]))
    if first:
        red[7 * r :, :] = jnp.zeros((r, k), jnp.float32)
    else:
        red[7 * r :, :] = sofar[0][7 * r :, :]
    if last:
        core = lax.axis_index("core")
        half = 4 * r
        sums[0][...] = red[pl.ds(pl.multiple_of(core * half, half), half), :]
        sums[1][...] = red[pl.ds(pl.multiple_of((1 - core) * half, half), half), :]
    else:
        sums[0][...] = red[...]
    for copy in outward:
        copy.wait()


def grams(base, sketch, archive, parts, sofar, last):
    first = not sofar
    k, r = max(sketch.shape), min(sketch.shape)
    rows, step = parts[0].shape
    halves = ((pltpu.HBM if first else pltpu.VMEM)((4 * k, step), jnp.bfloat16),) * 2
    sums = (jax.ShapeDtypeStruct((4 * r if last else 8 * r, k), jnp.float32),) * (1 + last)
    ordered = (jax.ShapeDtypeStruct((k, r), jnp.float32),) * first
    return pl.pallas_call(
        functools.partial(gram_kernel, base, first, last),
        out_shape=sums + halves + ordered,
        in_specs=[VMEM] + [ANY] * 4 + [VMEM] * len(sofar),
        out_specs=(VMEM,) * len(sums) + (ANY if first else VMEM,) * 2 + (VMEM,) * first,
        scratch_shapes=[
            pltpu.VMEM((4, rows, step), jnp.float32),
            pltpu.VMEM((8 * r, k), jnp.float32),
            pltpu.SemaphoreType.DMA((6,)),
        ]
        + ([pltpu.VMEM((4 * k, step), jnp.bfloat16)] * 2 + [pltpu.VMEM((k, r), jnp.float32)]) * first,
        compiler_params=PARAMS,
        cost_estimate=pl.CostEstimate(flops=128 * k * k * step, bytes_accessed=48 * k * step, transcendentals=0),
        name="grams",
    )(sketch, in_space(archive, pltpu.HBM), *parts, *sofar)


def modes_kernel(count, mine_ref, other_ref, leaf_ref, merge_ref, *refs):
    highs, lows, outs, (red, total, early, sem) = refs[:count], refs[count : 2 * count], refs[2 * count : -4], refs[-4:]
    fetches = [pltpu.make_async_copy(s[0], early.at[i], sem.at[i]) for i, s in enumerate((highs, lows))]
    for fetch in fetches:
        fetch.start()
    t = lax.axis_index("tm")
    core = lax.axis_index("core")
    half = mine_ref.shape[0]
    red[pl.ds(pl.multiple_of(core * half, half), half), :] = mine_ref[...]
    red[pl.ds(pl.multiple_of((1 - core) * half, half), half), :] = other_ref[...]
    a, b = split(mm(*combine(red, leaf_ref[...], merge_ref[...])))

    def dot(a, b):
        return jnp.dot(a, b, preferred_element_type=jnp.float32)

    for fetch in fetches:
        fetch.wait()
    at = 0
    for high, low in zip((early.at[0], *highs[1:]), (early.at[1], *lows[1:])):
        step = high.shape[1]
        both = dot(jnp.concatenate([a, b], 0), high[...])
        total[:, at : at + step] = both[: a.shape[0]] + (both[a.shape[0] :] + dot(a, low[...]))
        at += step
    per = outs[0].shape[0]
    for d, out in enumerate(outs):
        out[...] = total[pl.ds(pl.multiple_of(lax.rem(t + d, 4) * per, per), per), :]


def modes(mine, other, leaf, merge, high, low):
    k, r = leaf.shape
    count, cells = len(high), sum(h.shape[1] for h in high)
    return pl.pallas_call(
        functools.partial(modes_kernel, count),
        out_shape=(jax.ShapeDtypeStruct((r // 4, cells), jnp.float32),) * 4,
        in_specs=[VMEM] * 4 + ([ANY] + [VMEM] * (count - 1)) * 2,
        out_specs=(VMEM,) * 4,
        scratch_shapes=[
            pltpu.VMEM((8 * r, k), jnp.float32),
            pltpu.VMEM((r, cells), jnp.float32),
            pltpu.VMEM((2, *high[0].shape), jnp.bfloat16),
            pltpu.SemaphoreType.DMA((2,)),
        ],
        compiler_params=PARAMS,
        name="modes",
    )(mine, other, leaf, merge, *(in_space(v, pltpu.VMEM if i else pltpu.HBM) for s in (high, low) for i, v in enumerate(s)))


def place_kernel(p0, p1, p2, p3, out_ref, sem):
    t = lax.axis_index("tm")
    cells = p0.shape[1]
    copies = []
    for d, part in enumerate((p0, p1, p2, p3)):
        at = pl.multiple_of(lax.rem(t + 4 - d, 4) * cells, cells)
        copies.append(pltpu.make_async_copy(part, out_ref.at[:, pl.ds(at, cells)], sem.at[d]))
    for copy in copies:
        copy.start()
    for copy in copies:
        copy.wait()


def place(parts):
    rows, cells = parts[0].shape
    return pl.pallas_call(
        place_kernel,
        out_shape=jax.ShapeDtypeStruct((rows, 4 * cells), jnp.float32),
        in_specs=[ANY] * 4,
        out_specs=ANY,
        scratch_shapes=[pltpu.SemaphoreType.DMA((4,))],
        compiler_params=PARAMS,
        name="place",
    )(*parts)


def ring(axis, step):
    n = lax.axis_size(axis)
    return [(i, (i + step) % n) for i in range(n)]


def a2a(v, axis):
    return lax.all_to_all(v, axis, 0, 0, tiled=True)


def spread_over(v, axis):
    n = lax.axis_size(axis)
    return a2a(jnp.broadcast_to(v[None], (n, *v.shape)), axis)


def sum_everywhere(mine, theirs):
    rows, lanes = mine.shape
    outer, inner = ("x", "tm"), "z"
    n = lax.axis_size(outer)
    v = mine + lax.ppermute(theirs, "core", ring("core", 1))
    v = a2a(v.reshape(n, rows // n, lanes), outer).sum(0)
    v = spread_over(v, inner).sum(0)
    v = spread_over(v, outer).reshape(rows, lanes)
    return v, lax.ppermute(v, "core", ring("core", 1))


def on_device(archive, leaf, merge):
    r = leaf.shape[1]
    n = lax.axis_size("tm")
    t = lax.axis_index("tm")
    cells = archive.shape[1] // n
    sends = (2, 1, 3)
    bases = [sum(CHUNKS[:c]) for c in range(len(CHUNKS))]
    last = len(CHUNKS) - 1

    def send(c, source):
        at = [(t + d) % n * cells + bases[c] for d in sends]
        pieces = [lax.dynamic_slice_in_dim(source, a, CHUNKS[c], 1) for a in at]
        arrived = {d: lax.ppermute(p, "tm", ring("tm", d)) for d, p in zip(sends, pieces)}
        return [arrived[d] for d in (1, 2, 3)]

    source = archive
    moved = [send(0, source)]
    source, marker = lax.optimization_barrier((source, leaf))
    moved.append(send(1, source))
    sums, high, low, sketch = [], [], [], marker.T
    for c in range(last):
        if c + 2 <= last:
            source, *moved[c] = lax.optimization_barrier((source, *moved[c]))
            moved.append(send(c + 2, source))
        if c == 0:
            total, h, l, sketch = grams(bases[c], sketch, archive, moved[c], sums, False)
        else:
            total, h, l = grams(bases[c], sketch, archive, moved[c], sums, False)
        source, total = lax.optimization_barrier((source, total))
        sums = [total]
        high.append(h)
        low.append(l)
    *sums, h, l = grams(bases[last], sketch, archive, moved[last], sums, True)
    out = modes(*sum_everywhere(*sums), sketch, merge.T, [*high, h], [*low, l])
    back = {d: lax.ppermute(out[d], "tm", ring("tm", d)) for d in (1, 3, 2)}
    return place([out[0], *(back[d] for d in (1, 2, 3))])


def solution(mesh):
    fine = Mesh(mesh.devices.reshape(mesh.devices.shape[0] // 8, 4, 2, 4), (*SPACE, "tm"))
    return jax.shard_map(
        on_device, mesh=fine, in_specs=(P("tm", SPACE), P(), P()), out_specs=P("tm", SPACE), check_vma=False
    )
```

```python
import functools

import jax
import jax.numpy as jnp
from jax import lax
from jax.experimental import pallas as pl
from jax.experimental.pallas import tpu as pltpu
from jax.sharding import Mesh, PartitionSpec as P

HI = lax.Precision.HIGHEST
SUB = 8
VMEM = pl.BlockSpec(memory_space=pltpu.VMEM)
ANY = pl.BlockSpec(memory_space=pl.ANY)
in_space = pltpu.with_memory_space_constraint
SPACE = ("z", "x", "core")
PARAMS = pltpu.CompilerParams(vmem_limit_bytes=12 * 2**20)
CHUNKS = (512, 512, 768, 256)
PLAN = (((16, True), (16, True)), ((8, False), (16, False)), ((16, False), (16, False)))


def mm(a, b):
    return jnp.dot(a, b, precision=HI, preferred_element_type=jnp.float32)


def mmt(a, b):
    return lax.dot_general(a, b, (((1,), (1,)), ((), ())), precision=HI, preferred_element_type=jnp.float32)


def mtm(a, b):
    return lax.dot_general(a, b, (((0,), (0,)), ((), ())), precision=HI, preferred_element_type=jnp.float32)


def eliminate(mats, width, product, packed=False):
    n, lanes = mats[0].shape
    count = n // SUB
    rows = lax.broadcasted_iota(jnp.int32, (SUB, lanes), 0)
    left = lax.broadcasted_iota(jnp.int32, (SUB, lanes), 1) < n
    work = [[m[b * SUB : (b + 1) * SUB, :] for b in range(count)] for m in mats]

    def row(v, c):
        return jnp.broadcast_to(v[c : c + 1, :], (SUB, lanes))

    def column(v, c):
        wide = jnp.broadcast_to(v[:, c : c + 1], (SUB, lanes))
        if not packed:
            return wide
        return jnp.where(left, wide, jnp.broadcast_to(v[:, n + c : n + c + 1], (SUB, lanes)))

    for first in range(0, n, width):
        lo, hi = first // SUB, (first + width + SUB - 1) // SUB
        end = hi if product else count
        spread = [
            [{b: column(w[b], first + c) for b in range((first + c) // SUB, end)} for c in range(width)] for w in work
        ]
        pivots = [[] for _ in mats]
        for c in range(width):
            p, at = divmod(first + c, SUB)
            for w, t, d in zip(work, spread, pivots):
                d.append(row(t[c][p], at))
                inverse = 1.0 / d[c]
                pivot_row = row(w[p], at) * inverse
                for later in range(c + 1, width):
                    lp, lat = divmod(first + later, SUB)
                    scale = row(t[c][lp], lat) * inverse
                    for b in range(lp, end):
                        t[later][b] = t[later][b] - t[c][b] * scale
                w[p] = w[p] - jnp.where(rows > at, t[c][p], 0.0) * pivot_row
                for b in range(p + 1, end):
                    w[b] = w[b] - t[c][b] * pivot_row
        for w, d in zip(work, pivots):
            for b in range(lo, hi):
                scale = d[(b - lo) * SUB]
                for at in range(1, SUB):
                    scale = jnp.where(rows >= at, d[(b - lo) * SUB + at], scale)
                w[b] = w[b] * lax.rsqrt(scale)
            if product and hi < count:
                top = jnp.concatenate(w[lo:hi], 0)
                if packed:
                    below = jnp.concatenate([mtm(top[:, :n], top[:, :n]), mtm(top[:, n:], top[:, n:])], 1)
                else:
                    below = mtm(top[:, :n], top)
                for b in range(hi, count):
                    w[b] = w[b] - below[b * SUB : (b + 1) * SUB, :]
    return [jnp.concatenate(w, 0) for w in work]


def factor(sketched, grams, plan):
    r = sketched[0].shape[0]
    row = lax.broadcasted_iota(jnp.int32, (r, r), 0)
    lane = lax.broadcasted_iota(jnp.int32, (r, r), 1)
    eye = (row == lane).astype(jnp.float32)
    whole = eliminate([jnp.concatenate([s, eye], 1) for s in sketched], *plan[0])
    inverse = [e[:, r:] for e in whole]
    mixed = [mm(i, b) for i, b in zip(inverse, grams)]
    inner = [mmt(m, m) for m in mixed]
    if len(inner) > 1:
        both = [jnp.concatenate(inner[i : i + 2], 1) for i in range(0, len(inner), 2)]
        both = eliminate(both, *plan[1], packed=True)
        upper = [half for e in both for half in (e[:, :r], e[:, r:])]
    else:
        upper = eliminate(inner, *plan[1])
    return inverse, [jnp.where(lane >= row, u, 0.0) for u in upper]


def stack_pair(upper, maps, cross, sketch_t):
    ua, ub = upper
    r = ua.shape[0]
    va, vb = mm(sketch_t[:, :r], ua), mm(sketch_t[:, r:], ub)
    ta, tb = va + mmt(vb, cross), vb + mm(va, cross)
    sketched = mmt(ta, va) + mmt(tb, vb)
    gram = jnp.concatenate([mmt(ta, ua), mmt(tb, ub)], 1)
    return sketched, gram, jnp.concatenate([mm(va, maps[0]), mm(vb, maps[1])], 1)


def combine(red_ref, wl, wmt):
    r = wl.shape[1]
    grams = [red_ref[w * r : (w + 1) * r, :] for w in range(4)]
    z, u = factor([mm(g, wl) for g in grams], grams, PLAN[0])
    pairs = []
    for i in range(2):
        cross = mmt(mm(z[2 * i], red_ref[4 * r : 5 * r, i * r : (i + 1) * r]), z[2 * i + 1])
        pairs.append(stack_pair(u[2 * i : 2 * i + 2], z[2 * i : 2 * i + 2], cross, wmt))
    inverse, u = factor([p[0] for p in pairs], [p[1] for p in pairs], PLAN[1])
    z = [mm(i, p[2]) for i, p in zip(inverse, pairs)]
    cross = mmt(mm(z[0], red_ref[5 * r : 7 * r, :]), z[1])
    sketched, gram, rows = stack_pair(u, z, cross, wmt)
    inverse, u = factor([sketched], [gram], PLAN[2])
    z = mm(inverse[0], rows)
    return u[0], jnp.concatenate([mmt(z[:, w * r : (w + 1) * r], wl) for w in range(4)], 1)


def dot_rows(a, b):
    return lax.dot_general(a, b, (((1,), (1,)), ((), ())), preferred_element_type=jnp.float32)


def split(x):
    high = x.astype(jnp.bfloat16)
    return high, (x - high.astype(jnp.float32)).astype(jnp.bfloat16)


def store_halves(t, d, rows_ref, high_ref, low_ref):
    per = rows_ref.shape[0] // 4
    for w in range(4):
        at = pl.ds(pl.multiple_of(w * 4 * per + lax.rem(t + 4 - d, 4) * per, per), per)
        high_ref[at, :], low_ref[at, :] = split(rows_ref[w * per : (w + 1) * per, :])


def own_cells(archive_ref, t, base, step):
    at = pl.multiple_of(t * (archive_ref.shape[1] // 4) + base, 128)
    return archive_ref.at[:, pl.ds(at, step)]


def gram_kernel(base, first, last, sketch_ref, archive_ref, p1, p2, p3, *refs):
    sofar, refs = refs[: not first], refs[not first :]
    sums, refs = refs[: 1 + last], refs[1 + last :]
    halves_out, refs = refs[:2], refs[2:]
    sketch_out, (held, red, sem, *extra) = refs[:first], refs[first:]
    high_ref, low_ref = extra[:2] if first else halves_out
    t = lax.axis_index("tm")
    step = held.shape[2]
    sources = (own_cells(archive_ref, t, base, step), p1, p2, p3)
    copies = [pltpu.make_async_copy(p, held.at[d], sem.at[d]) for d, p in enumerate(sources)]
    for copy in copies:
        copy.start()
    if first:
        k = sketch_ref.shape[1]
        extra[2][...] = sketch_ref[...].T
        wl = jnp.concatenate([extra[2][pl.ds(j, k // 4, stride=4), :] for j in range(4)], 0)
        sketch_out[0][...] = wl
    else:
        wl = sketch_ref[...]
    k, r = wl.shape
    for d, copy in enumerate(copies):
        copy.wait()
        store_halves(t, d, held.at[d], high_ref, low_ref)
    outward = [pltpu.make_async_copy(a, b, sem.at[4 + i]) for i, (a, b) in enumerate(zip(extra[:2], halves_out))]
    for copy in outward:
        copy.start()
    halves = [(ref[: 2 * k, :], ref[2 * k :, :]) for ref in (high_ref, low_ref)]

    def block(i, j):
        hi, li, hj, lj = halves[0][i], halves[1][i], halves[0][j], halves[1][j]
        return dot_rows(hi, hj) + (dot_rows(hi, lj) + dot_rows(li, hj) + dot_rows(li, lj))

    blank = jnp.zeros_like(wl)
    wide = jnp.concatenate([jnp.concatenate([wl, blank], 1), jnp.concatenate([blank, wl], 1)], 0)
    sketched = mm(jnp.concatenate([block(0, 0), block(1, 1), block(0, 1)], 0), wide)
    near = lax.broadcasted_iota(jnp.int32, (k, 2 * r), 1) < r

    def add(at, value):
        to = slice(at * r, at * r + value.shape[0])
        red[to, :] = value if first else sofar[0][to, :] + value

    beside = []
    for i in range(2):
        top, bottom = sketched[2 * i * k : (2 * i + 1) * k], sketched[(2 * i + 1) * k : (2 * i + 2) * k]
        add(2 * i, jnp.where(near, top, bottom).T)
        beside.append(top[:, r:])
    add(4, mtm(wl, jnp.concatenate(beside, 1)))
    add(5, mtm(wide, sketched[4 * k :]))
    if first:
        red[7 * r :, :] = jnp.zeros((r, k), jnp.float32)
    else:
        red[7 * r :, :] = sofar[0][7 * r :, :]
    if last:
        core = lax.axis_index("core")
        half = 4 * r
        sums[0][...] = red[pl.ds(pl.multiple_of(core * half, half), half), :]
        sums[1][...] = red[pl.ds(pl.multiple_of((1 - core) * half, half), half), :]
    else:
        sums[0][...] = red[...]
    for copy in outward:
        copy.wait()


def grams(base, sketch, archive, parts, sofar, last):
    first = not sofar
    k, r = max(sketch.shape), min(sketch.shape)
    rows, step = parts[0].shape
    halves = ((pltpu.HBM if first else pltpu.VMEM)((4 * k, step), jnp.bfloat16),) * 2
    sums = (jax.ShapeDtypeStruct((4 * r if last else 8 * r, k), jnp.float32),) * (1 + last)
    ordered = (jax.ShapeDtypeStruct((k, r), jnp.float32),) * first
    return pl.pallas_call(
        functools.partial(gram_kernel, base, first, last),
        out_shape=sums + halves + ordered,
        in_specs=[VMEM] + [ANY] * 4 + [VMEM] * len(sofar),
        out_specs=(VMEM,) * len(sums) + (ANY if first else VMEM,) * 2 + (VMEM,) * first,
        scratch_shapes=[
            pltpu.VMEM((4, rows, step), jnp.float32),
            pltpu.VMEM((8 * r, k), jnp.float32),
            pltpu.SemaphoreType.DMA((6,)),
        ]
        + ([pltpu.VMEM((4 * k, step), jnp.bfloat16)] * 2 + [pltpu.VMEM((k, r), jnp.float32)]) * first,
        compiler_params=PARAMS,
        cost_estimate=pl.CostEstimate(flops=128 * k * k * step, bytes_accessed=48 * k * step, transcendentals=0),
        name="grams",
    )(sketch, in_space(archive, pltpu.HBM), *parts, *sofar)


def modes_kernel(count, pieces, sum_ref, leaf_ref, merge_ref, *refs):
    highs, lows, outs, (red, total, early, sem) = refs[:count], refs[count : 2 * count], refs[2 * count : -4], refs[-4:]
    fetches = [pltpu.make_async_copy(s[0], early.at[i], sem.at[i]) for i, s in enumerate((highs, lows))]
    for fetch in fetches:
        fetch.start()
    t = lax.axis_index("tm")
    core = lax.axis_index("core")
    half = sum_ref.shape[0] // 2
    rows = half // pieces
    for i in range(pieces):
        for h, side in enumerate((core, 1 - core)):
            at = pl.multiple_of(side * half + i * rows, rows)
            red[pl.ds(at, rows), :] = sum_ref[(2 * i + h) * rows : (2 * i + h + 1) * rows, :]
    a, b = split(mm(*combine(red, leaf_ref[...], merge_ref[...])))

    def dot(a, b):
        return jnp.dot(a, b, preferred_element_type=jnp.float32)

    for fetch in fetches:
        fetch.wait()
    at = 0
    for high, low in zip((early.at[0], *highs[1:]), (early.at[1], *lows[1:])):
        step = high.shape[1]
        both = dot(jnp.concatenate([a, b], 0), high[...])
        total[:, at : at + step] = both[: a.shape[0]] + (both[a.shape[0] :] + dot(a, low[...]))
        at += step
    per = outs[0].shape[0]
    for d, out in enumerate(outs):
        out[...] = total[pl.ds(pl.multiple_of(lax.rem(t + d, 4) * per, per), per), :]


def modes(total, leaf, merge, high, low):
    k, r = leaf.shape
    count, cells = len(high), sum(h.shape[1] for h in high)
    return pl.pallas_call(
        functools.partial(modes_kernel, count, lax.axis_size(("x", "tm"))),
        out_shape=(jax.ShapeDtypeStruct((r // 4, cells), jnp.float32),) * 4,
        in_specs=[VMEM] * 3 + ([ANY] + [VMEM] * (count - 1)) * 2,
        out_specs=(VMEM,) * 4,
        scratch_shapes=[
            pltpu.VMEM((8 * r, k), jnp.float32),
            pltpu.VMEM((r, cells), jnp.float32),
            pltpu.VMEM((2, *high[0].shape), jnp.bfloat16),
            pltpu.SemaphoreType.DMA((2,)),
        ],
        compiler_params=PARAMS,
        name="modes",
    )(total, leaf, merge, *(in_space(v, pltpu.VMEM if i else pltpu.HBM) for s in (high, low) for i, v in enumerate(s)))


def place_kernel(p0, p1, p2, p3, out_ref, sem):
    t = lax.axis_index("tm")
    cells = p0.shape[1]
    copies = []
    for d, part in enumerate((p0, p1, p2, p3)):
        at = pl.multiple_of(lax.rem(t + 4 - d, 4) * cells, cells)
        copies.append(pltpu.make_async_copy(part, out_ref.at[:, pl.ds(at, cells)], sem.at[d]))
    for copy in copies:
        copy.start()
    for copy in copies:
        copy.wait()


def place(parts):
    rows, cells = parts[0].shape
    return pl.pallas_call(
        place_kernel,
        out_shape=jax.ShapeDtypeStruct((rows, 4 * cells), jnp.float32),
        in_specs=[ANY] * 4,
        out_specs=ANY,
        scratch_shapes=[pltpu.SemaphoreType.DMA((4,))],
        compiler_params=PARAMS,
        name="place",
    )(*parts)


def ring(axis, step):
    n = lax.axis_size(axis)
    return [(i, (i + step) % n) for i in range(n)]


def a2a(v, axis):
    return lax.all_to_all(v, axis, 0, 0, tiled=True)


def spread_over(v, axis):
    n = lax.axis_size(axis)
    return a2a(jnp.broadcast_to(v[None], (n, *v.shape)), axis)


def sum_everywhere(mine, theirs):
    rows, lanes = mine.shape
    outer, inner = ("x", "tm"), "z"
    n = lax.axis_size(outer)
    v = mine + lax.ppermute(theirs, "core", ring("core", 1))
    v = a2a(v.reshape(n, rows // n, lanes), outer).sum(0)
    v = spread_over(v, inner).sum(0)
    other = lax.ppermute(v, "core", ring("core", 1))
    return spread_over(jnp.concatenate([v, other], 0), outer).reshape(2 * rows, lanes)


def on_device(archive, leaf, merge):
    r = leaf.shape[1]
    n = lax.axis_size("tm")
    t = lax.axis_index("tm")
    cells = archive.shape[1] // n
    sends = (2, 1, 3)
    bases = [sum(CHUNKS[:c]) for c in range(len(CHUNKS))]
    last = len(CHUNKS) - 1

    def send(c, source):
        at = [(t + d) % n * cells + bases[c] for d in sends]
        pieces = [lax.dynamic_slice_in_dim(source, a, CHUNKS[c], 1) for a in at]
        arrived = {d: lax.ppermute(p, "tm", ring("tm", d)) for d, p in zip(sends, pieces)}
        return [arrived[d] for d in (1, 2, 3)]

    source = archive
    moved = [send(0, source)]
    source, marker = lax.optimization_barrier((source, leaf))
    moved.append(send(1, source))
    sums, high, low, sketch = [], [], [], marker.T
    for c in range(last):
        if c + 2 <= last:
            source, *moved[c] = lax.optimization_barrier((source, *moved[c]))
            moved.append(send(c + 2, source))
        if c == 0:
            total, h, l, sketch = grams(bases[c], sketch, archive, moved[c], sums, False)
        else:
            total, h, l = grams(bases[c], sketch, archive, moved[c], sums, False)
        source, total = lax.optimization_barrier((source, total))
        sums = [total]
        high.append(h)
        low.append(l)
    *sums, h, l = grams(bases[last], sketch, archive, moved[last], sums, True)
    out = modes(sum_everywhere(*sums), sketch, merge.T, [*high, h], [*low, l])
    back = {d: lax.ppermute(out[d], "tm", ring("tm", d)) for d in (1, 3, 2)}
    return place([out[0], *(back[d] for d in (1, 2, 3))])


def solution(mesh):
    fine = Mesh(mesh.devices.reshape(mesh.devices.shape[0] // 8, 4, 2, 4), (*SPACE, "tm"))
    return jax.shard_map(
        on_device, mesh=fine, in_specs=(P("tm", SPACE), P(), P()), out_specs=P("tm", SPACE), check_vma=False
    )
```
